32 devices in a mesh: gy: 4 (over z), gz: 8 (over y, x, core).
Axes of the slice: x: 2, y: 2, z: 4, core: 2. Of those that a mesh axis runs over, the one named last changes fastest.
Arguments:
- snapshots: float32 [16, 3, 1, 512, 512], P(None, None, None, 'gz', 'gy'), may hold values from -6 to 6
- cell_weight: float32 [512], P('gy'), may hold values from 0.4 to 7.5, as said below
Outputs:
- pod_modes: float32 [16, 3, 1, 512, 512], P(None, None, None, 'gz', 'gy')
- factor: float32 [16, 16], replicated
The draws below stay inside these ranges and needn't reach their ends.
Inputs may be any that keep to these rules, and one draw needn't show every extreme that they name: `cell_weight`: weights are positive.
All inputs are finite; a program needn't handle non-finite values.
Results may differ from the reference program's by a relative error of at most 0.000071.
Values sent between devices are 32-bit elements; how exact they have to be, the bound alone decides.
A program may use at most 64 MiB of HBM per device.

```python
import math
import jax
import jax.numpy as jnp
from jax import lax

SNAP = 16
PX = 1
NY = 512
NZ = 512


def draw_cell_weight(key, part):
    key = jax.random.fold_in(key, 7)
    position = jnp.arange(NY, dtype=jnp.float32) / float(max(NY - 1, 1))
    trend = jnp.exp(math.log(3.0) * position)
    rough = jnp.exp(jax.random.uniform(key, (NY,), jnp.float32, math.log(0.5), math.log(2.0)))
    return jnp.clip(trend * rough, 0.4, 7.5)


def levels(rng, extent, split, smallest, top_value):
    def one(dim, parts):
        draws = jax.random.uniform(jax.random.fold_in(jax.random.fold_in(rng, 6), dim), (parts,), jnp.float32, smallest / len(split), top_value / len(split))
        return jnp.repeat(jnp.exp(draws), extent[dim] // parts).reshape((-1,) + (1,) * (len(extent) - dim - 1))

    factor_of = one(*split[0])
    for cut in split[1:]:
        factor_of = factor_of * one(*cut)
    return factor_of


def gaussian(rng, dims, width, most, split=(), held_as=jnp.bfloat16):
    result = width * jax.random.normal(rng, dims, jnp.float32)
    if split:
        result = result * levels(rng, dims, split, -0.22, 0.18)
    return jnp.clip(result, -most, most).astype(held_as)


def setup_inputs(seed: int = 0) -> dict:
    key_list = jax.random.split(jax.random.key(seed), 3)
    return {
        "snapshots": gaussian(key_list[0], (SNAP, 3, PX, NZ, NY), 1.0, 6.0, ((3, 8), (4, 4)), jnp.float32),
        "cell_weight": draw_cell_weight(jax.random.fold_in(key_list[2], 71), 0),
    }


FILTER_RAW = [math.exp(-(offset - 4) * (offset - 4) / 4.5) for offset in range(9)]
FILTER_TAPS = [value / sum(FILTER_RAW) for value in FILTER_RAW]

def smooth_one(field):
    padded = jnp.pad(field, ((0, 0), (0, 0), (0, 0), (4, 4)))
    along_y = sum((FILTER_TAPS[offset] * padded[..., offset:offset + NY] for offset in range(9)))
    wrapped = jnp.concatenate([along_y[:, :, NZ - 4:, :], along_y, along_y[:, :, :4, :]], axis=2)
    return sum((FILTER_TAPS[offset] * wrapped[:, :, offset:offset + NZ, :] for offset in range(9)))

def reference(snapshots, cell_weight):
    smoothed = lax.map(smooth_one, snapshots)
    weighted = smoothed * jnp.sqrt(cell_weight)[None, None, None, None, :]
    flat_rows = weighted.reshape(SNAP, -1)
    gram_local = jnp.dot(flat_rows.astype(jnp.float32), flat_rows.T.astype(jnp.float32), precision=lax.Precision.HIGHEST, preferred_element_type=jnp.float32)
    upper_factor = jnp.linalg.cholesky(gram_local).T
    row_total = 3 * PX * NY * NZ
    basis_rows = lax.linalg.triangular_solve(upper_factor.T, flat_rows, left_side=True, lower=True)
    pod_modes = (basis_rows * math.sqrt(row_total)).reshape(snapshots.shape)
    return (pod_modes, upper_factor / math.sqrt(row_total))
```

```python
import functools
import math

import jax
import jax.numpy as jnp
from jax import lax
from jax.experimental import pallas as pl
from jax.experimental.pallas import tpu as pltpu
from jax.sharding import PartitionSpec as P

FILTER_RAW = [math.exp(-(offset - 4) * (offset - 4) / 4.5) for offset in range(9)]
FILTER_TAPS = [value / sum(FILTER_RAW) for value in FILTER_RAW]
HALF_TAPS = FILTER_TAPS[4:]

MESH = pl.DeviceIdType.MESH
F32, BF16 = jnp.float32, jnp.bfloat16


def split(value):
    high = value.astype(BF16)
    return high, (value - high.astype(F32)).astype(BF16)


def band(distance):
    out = jnp.zeros(distance.shape, F32)
    for k in range(5):
        out = jnp.where(distance == k, HALF_TAPS[k], out)
    return out


def lane_roll(value, shift):
    flat = value.reshape(-1, value.shape[-1])
    return pltpu.roll(flat, shift, 1).reshape(value.shape)


def filter_z(ref, index, cells):
    out = HALF_TAPS[0] * ref[index, pl.ds(8, cells), :]
    for k in range(1, 5):
        out = out + HALF_TAPS[k] * (
            ref[index, pl.ds(8 - k, cells), :] + ref[index, pl.ds(8 + k, cells), :]
        )
    return out


def kernel(
    snaps, comps, row_total, x_ref, w_ref, modes_ref, factor_ref,
    field, pack_low, pack_high, side, corner, halo, rows, gram_z, gram_y,
    load_sem, halo_send, halo_recv, gz_send, gz_recv, gy_send, gy_recv,
):
    cells, width = x_ref.shape[1], x_ref.shape[2]
    half = cells // 2
    gy, gz = lax.axis_index("gy"), lax.axis_index("gz")
    ny, nz = lax.axis_size("gy"), lax.axis_size("gz")

    def gz_at(step):
        return lax.rem(gz + step + nz, nz)

    loads = []
    part = snaps * comps // 4
    for q in range(4):
        loads.append(pltpu.make_async_copy(
            x_ref.at[pl.ds(q * part, part)],
            field.at[pl.ds(q * part, part), pl.ds(8, cells)],
            load_sem.at[q],
        ))
        loads[-1].start()
    side[...] = jnp.zeros_like(side)
    corner[...] = jnp.zeros_like(corner)

    barrier = pltpu.get_barrier_semaphore()
    peers = [(gy, gz_at(d)) for d in range(1, nz)]
    peers += [(lax.rem(gy + d, ny), gz) for d in range(1, ny)]
    for d in (1, -1):
        peers += [(lax.rem(gy + d + ny, ny), gz_at(1)), (lax.rem(gy + d + ny, ny), gz_at(-1))]
    for peer in peers:
        pl.semaphore_signal(barrier, inc=1, device_id=peer, device_id_type=MESH)

    lane = lax.broadcasted_iota(jnp.int32, (1, width), 1)
    packed = jnp.zeros((comps * cells, width), F32)
    for s in range(snaps):
        if s % 4 == 0:
            loads[s // 4].wait()
        block = field[pl.ds(comps * s, comps), pl.ds(8, cells), :].reshape(comps * cells, width)
        packed = jnp.where(lane // 8 == s, pltpu.roll(block, (4 + 8 * s) % width, 1), packed)
    packed = packed.reshape(comps, cells, width)
    first, second = packed[:, :half], packed[:, half:]
    left_lanes = (lane % 8 < 4).reshape(1, 1, width)
    pack_high[...] = jnp.where(left_lanes, first, lane_roll(second, 4))
    pack_low[...] = jnp.where(left_lanes, lane_roll(second, width - 4), first)

    pl.semaphore_wait(barrier, len(peers))

    def remote(src, dst, n, target):
        return pltpu.make_async_remote_copy(
            src_ref=src, dst_ref=dst, send_sem=halo_send.at[n], recv_sem=halo_recv.at[n],
            device_id=target, device_id_type=MESH,
        )

    copies = [
        remote(x_ref.at[:, pl.ds(cells - 4, 4), :], field.at[:, pl.ds(4, 4), :], 0, (gy, gz_at(1))),
        remote(x_ref.at[:, pl.ds(0, 4), :], field.at[:, pl.ds(cells + 8, 4), :], 1, (gy, gz_at(-1))),
    ]
    up = jnp.minimum(gy + 1, ny - 1)
    down = jnp.maximum(gy - 1, 0)
    to_up = [
        remote(pack_high, side.at[0], 2, (up, gz)),
        remote(pack_high.at[:, pl.ds(half - 8, 8)], corner.at[0, 0], 3, (up, gz_at(1))),
        remote(pack_high.at[:, pl.ds(0, 8)], corner.at[0, 1], 4, (up, gz_at(-1))),
    ]
    to_down = [
        remote(pack_low, side.at[1], 5, (down, gz)),
        remote(pack_low.at[:, pl.ds(half - 8, 8)], corner.at[1, 0], 6, (down, gz_at(1))),
        remote(pack_low.at[:, pl.ds(0, 8)], corner.at[1, 1], 7, (down, gz_at(-1))),
    ]

    @pl.when(gy < ny - 1)
    def _():
        for copy in to_up:
            copy.start()

    @pl.when(gy > 0)
    def _():
        for copy in to_down:
            copy.start()

    for copy in copies:
        copy.start()

    root = jnp.sqrt(w_ref[...])
    row_i = lax.broadcasted_iota(jnp.int32, (width, width), 0)
    col_i = lax.broadcasted_iota(jnp.int32, (width, width), 1)
    j = row_i % 8
    position = jnp.where(j < 4, j - 4, width + j - 4)
    matrix = jnp.concatenate(
        [band(jnp.abs(row_i - col_i)) * root, band(jnp.abs(position - col_i)) * root], axis=0
    )
    matrix_high, matrix_low = split(matrix)
    matrix_both = jnp.concatenate([matrix_high, matrix_low], axis=1)

    @pl.when(gy > 0)
    def _():
        for copy in to_up:
            copy.wait_recv()

    @pl.when(gy < ny - 1)
    def _():
        for copy in to_down:
            copy.wait_recv()

    halo[:, pl.ds(0, 8), :] = jnp.where(
        left_lanes, lane_roll(corner[0, 0], width - 4), lane_roll(corner[1, 0], 4))
    halo[:, pl.ds(8, half), :] = jnp.where(left_lanes, side[0], side[1])
    halo[:, pl.ds(8 + half, half), :] = jnp.where(
        left_lanes, lane_roll(side[0], width - 4), lane_roll(side[1], 4))
    halo[:, pl.ds(8 + cells, 8), :] = jnp.where(left_lanes, corner[0, 1], corner[1, 1])
    halo_z = jnp.concatenate([filter_z(halo, c, cells) for c in range(comps)], axis=0)
    halo_high, halo_low = split(halo_z)

    for copy in copies:
        copy.wait_recv()

    def smooth_one(s, carry):
        field_z = jnp.concatenate(
            [filter_z(field, comps * s + c, cells) for c in range(comps)], axis=0)
        high, low = split(field_z)
        keep = (lane // 8 == s).astype(F32).astype(BF16)
        left = jnp.dot(
            jnp.concatenate([high, halo_high * keep], axis=1), matrix_both,
            preferred_element_type=F32)
        right = jnp.dot(
            jnp.concatenate([low, halo_low * keep], axis=1), matrix_high,
            preferred_element_type=F32)
        high, low = split(left[:, :width] + left[:, width:] + right)
        for n in range(comps * cells // 16):
            rows[s, :, pl.ds(2 * width * n, width)] = high[16 * n:16 * n + 16]
            rows[s, :, pl.ds(2 * width * n + width, width)] = low[16 * n:16 * n + 16]
        return carry

    lax.fori_loop(0, snaps, smooth_one, 0)

    chunks = comps * cells // 16
    size = snaps * 16
    both = rows[...].reshape(size, 2 * width * chunks)
    swapped = jnp.concatenate(
        [both[:, width * (n ^ 1):width * (n ^ 1) + width] for n in range(2 * chunks)], axis=1)
    dims = (((1,), (1,)), ((), ()))
    big = lax.dot_general(both, both, dims, preferred_element_type=F32)
    big = big + lax.dot_general(swapped, both, dims, preferred_element_type=F32)
    big_i = lax.broadcasted_iota(jnp.int32, (size, size), 0)
    big_j = lax.broadcasted_iota(jnp.int32, (size, size), 1)
    same = big_i % 16 == big_j % 16
    big = jnp.where(same, big, 0.0).reshape(snaps, 16, size).sum(axis=1)
    gather_i = lax.broadcasted_iota(jnp.int32, (size, width), 0)
    gather_j = lax.broadcasted_iota(jnp.int32, (size, width), 1)
    gather = (gather_i // 16 == gather_j).astype(F32)
    gram = jnp.dot(big, gather, precision=lax.Precision.HIGHEST, preferred_element_type=F32)

    def all_sum(value, slots, mine, count, send, recv, device):
        slots[mine] = value
        sent = []
        for d in range(1, count):
            copy = pltpu.make_async_remote_copy(
                src_ref=slots.at[mine], dst_ref=slots.at[mine],
                send_sem=send.at[d], recv_sem=recv.at[d],
                device_id=device(lax.rem(mine + d, count)), device_id_type=MESH,
            )
            copy.start()
            sent.append(copy)
        for copy in sent:
            copy.wait_recv()
        total = slots[0]
        for n in range(1, count):
            total = total + slots[n]
        return total, sent

    gram, sent_z = all_sum(gram, gram_z, gz, nz, gz_send, gz_recv, lambda n: (gy, n))
    gram, sent_y = all_sum(gram, gram_y, gy, ny, gy_send, gy_recv, lambda n: (n, gz))

    m_i = lax.broadcasted_iota(jnp.int32, (snaps, width), 0)
    m_j = lax.broadcasted_iota(jnp.int32, (snaps, width), 1)
    work = jnp.where(m_j == m_i + snaps, 1.0, gram)
    for k in range(snaps - 1):
        scaled = work[k:k + 1, :] / work[k:k + 1, k:k + 1]
        work = work - jnp.where(m_i > k, work[:, k:k + 1], 0.0) * scaled
    pivots = jnp.sum(jnp.where(m_i == m_j, work, 0.0), axis=1, keepdims=True)
    work = work / jnp.sqrt(pivots)
    upper = jnp.where(m_j >= m_i, work, 0.0) * (1.0 / math.sqrt(row_total))
    factor_ref[...] = upper[:, :snaps]

    inverse_high, inverse_low = split(work * math.sqrt(row_total))
    spread_i = lax.broadcasted_iota(jnp.int32, (width, size), 0)
    spread_j = lax.broadcasted_iota(jnp.int32, (width, size), 1)
    spread = (spread_i - snaps == spread_j // 16).astype(F32).astype(BF16)

    def blocks(value):
        tall = jnp.broadcast_to(
            value.astype(F32)[:, None, :], (snaps, 16, width)).reshape(size, width).astype(BF16)
        wide = jnp.dot(tall, spread, preferred_element_type=F32)
        return jnp.where(same, wide, 0.0).astype(BF16)

    inverse_high, inverse_low = blocks(inverse_high), blocks(inverse_low)
    for n in range(chunks):
        block = rows[:, :, pl.ds(2 * width * n, 2 * width)].reshape(size, 2 * width)
        left = jnp.dot(inverse_high, block, preferred_element_type=F32)
        right = jnp.dot(inverse_low, block[:, :width], preferred_element_type=F32)
        out = left[:, :width] + left[:, width:] + right
        modes_ref[:, pl.ds(16 * n, 16), :] = out.reshape(snaps, 16, width)

    for copy in copies + sent_z + sent_y:
        copy.wait_send()

    @pl.when(gy < ny - 1)
    def _():
        for copy in to_up:
            copy.wait_send()

    @pl.when(gy > 0)
    def _():
        for copy in to_down:
            copy.wait_send()


def per_device(snapshots, cell_weight):
    snaps, comps, planes, cells, width = snapshots.shape
    comps_all = comps * planes
    ny, nz = lax.axis_size("gy"), lax.axis_size("gz")
    row_total = comps_all * cells * width * ny * nz
    modes, factor = pl.pallas_call(
        functools.partial(kernel, snaps, comps_all, row_total),
        out_shape=(
            jax.ShapeDtypeStruct((snaps, comps_all * cells, width), F32),
            jax.ShapeDtypeStruct((snaps, snaps), F32),
        ),
        in_specs=[pl.BlockSpec(memory_space=pl.ANY), pl.BlockSpec(memory_space=pltpu.VMEM)],
        out_specs=(
            pl.BlockSpec(memory_space=pltpu.VMEM),
            pl.BlockSpec(memory_space=pltpu.VMEM),
        ),
        scratch_shapes=[
            pltpu.VMEM((snaps * comps_all, cells + 16, width), F32),
            pltpu.VMEM((comps_all, cells // 2, width), F32),
            pltpu.VMEM((comps_all, cells // 2, width), F32),
            pltpu.VMEM((2, comps_all, cells // 2, width), F32),
            pltpu.VMEM((2, 2, comps_all, 8, width), F32),
            pltpu.VMEM((comps_all, cells + 16, width), F32),
            pltpu.VMEM((snaps, 16, 2 * width * comps_all * cells // 16), BF16),
            pltpu.VMEM((nz, snaps, width), F32),
            pltpu.VMEM((ny, snaps, width), F32),
            pltpu.SemaphoreType.DMA((4,)),
            pltpu.SemaphoreType.DMA((8,)),
            pltpu.SemaphoreType.DMA((8,)),
            pltpu.SemaphoreType.DMA((nz,)),
            pltpu.SemaphoreType.DMA((nz,)),
            pltpu.SemaphoreType.DMA((ny,)),
            pltpu.SemaphoreType.DMA((ny,)),
        ],
        compiler_params=pltpu.CompilerParams(
            collective_id=0, has_side_effects=True, vmem_limit_bytes=40 * 1024 * 1024
        ),
    )(snapshots.reshape(snaps * comps_all, cells, width), cell_weight.reshape(1, width))
    return modes.reshape(snapshots.shape), factor


def solution(mesh):
    return jax.shard_map(
        per_device,
        mesh=mesh,
        in_specs=(P(None, None, None, "gz", "gy"), P("gy")),
        out_specs=(P(None, None, None, "gz", "gy"), P()),
        check_vma=False,
    )
```

```python
import functools
import math

import jax
import jax.numpy as jnp
from jax import lax
from jax.experimental import pallas as pl
from jax.experimental.pallas import tpu as pltpu
from jax.sharding import PartitionSpec as P

FILTER_RAW = [math.exp(-(offset - 4) * (offset - 4) / 4.5) for offset in range(9)]
FILTER_TAPS = [value / sum(FILTER_RAW) for value in FILTER_RAW]
HALF_TAPS = FILTER_TAPS[4:]

MESH = pl.DeviceIdType.MESH
F32, BF16 = jnp.float32, jnp.bfloat16


def split(value):
    high = value.astype(BF16)
    return high, (value - high.astype(F32)).astype(BF16)


def band(distance):
    out = jnp.zeros(distance.shape, F32)
    for k in range(5):
        out = jnp.where(distance == k, HALF_TAPS[k], out)
    return out


def lane_roll(value, shift):
    flat = value.reshape(-1, value.shape[-1])
    return pltpu.roll(flat, shift, 1).reshape(value.shape)


def filter_z(ref, index, cells):
    out = HALF_TAPS[0] * ref[index, pl.ds(8, cells), :]
    for k in range(1, 5):
        out = out + HALF_TAPS[k] * (
            ref[index, pl.ds(8 - k, cells), :] + ref[index, pl.ds(8 + k, cells), :]
        )
    return out


def rows_kernel(
    snaps, comps, x_ref, w_ref, rows_high, rows_low, gram_ref,
    field, weight, pack_low, pack_high, side, corner, halo, square, slots,
    load_sem, halo_send, halo_recv, gram_send, gram_recv,
):
    cells, width = x_ref.shape[1], x_ref.shape[2]
    half = cells // 2
    gy, gz = lax.axis_index("gy"), lax.axis_index("gz")
    ny, nz = lax.axis_size("gy"), lax.axis_size("gz")

    def gz_at(step):
        return lax.rem(gz + step + nz, nz)

    loads = []
    part = snaps * comps // 4
    for q in range(4):
        loads.append(pltpu.make_async_copy(
            x_ref.at[pl.ds(q * part, part)],
            field.at[pl.ds(q * part, part), pl.ds(8, cells)],
            load_sem.at[q],
        ))
        loads[-1].start()
    load_weight = pltpu.make_async_copy(w_ref, weight, load_sem.at[4])
    load_weight.start()
    side[...] = jnp.zeros_like(side)
    corner[...] = jnp.zeros_like(corner)

    barrier = pltpu.get_barrier_semaphore()
    devices = ny * nz
    mine = gy * nz + gz

    def device_at(step):
        flat = lax.rem(mine + step, devices)
        return flat // nz, lax.rem(flat, nz)

    def greet(step, carry):
        pl.semaphore_signal(barrier, inc=1, device_id=device_at(step), device_id_type=MESH)
        return carry

    lax.fori_loop(1, devices, greet, 0, unroll=devices <= 64)

    lane = lax.broadcasted_iota(jnp.int32, (1, width), 1)
    packed = jnp.zeros((comps * cells, width), F32)
    for s in range(snaps):
        if s % 4 == 0:
            loads[s // 4].wait()
        block = field[pl.ds(comps * s, comps), pl.ds(8, cells), :].reshape(comps * cells, width)
        packed = jnp.where(lane // 8 == s, pltpu.roll(block, (4 + 8 * s) % width, 1), packed)
    packed = packed.reshape(comps, cells, width)
    first, second = packed[:, :half], packed[:, half:]
    left_lanes = (lane % 8 < 4).reshape(1, 1, width)
    pack_high[...] = jnp.where(left_lanes, first, lane_roll(second, 4))
    pack_low[...] = jnp.where(left_lanes, lane_roll(second, width - 4), first)

    pl.semaphore_wait(barrier, devices - 1)

    def remote(src, dst, n, target):
        return pltpu.make_async_remote_copy(
            src_ref=src, dst_ref=dst, send_sem=halo_send.at[n], recv_sem=halo_recv.at[n],
            device_id=target, device_id_type=MESH,
        )

    copies = [
        remote(x_ref.at[:, pl.ds(cells - 4, 4), :], field.at[:, pl.ds(4, 4), :], 0, (gy, gz_at(1))),
        remote(x_ref.at[:, pl.ds(0, 4), :], field.at[:, pl.ds(cells + 8, 4), :], 1, (gy, gz_at(-1))),
    ]
    up = jnp.minimum(gy + 1, ny - 1)
    down = jnp.maximum(gy - 1, 0)
    to_up = [
        remote(pack_high, side.at[0], 2, (up, gz)),
        remote(pack_high.at[:, pl.ds(half - 8, 8)], corner.at[0, 0], 3, (up, gz_at(1))),
        remote(pack_high.at[:, pl.ds(0, 8)], corner.at[0, 1], 4, (up, gz_at(-1))),
    ]
    to_down = [
        remote(pack_low, side.at[1], 5, (down, gz)),
        remote(pack_low.at[:, pl.ds(half - 8, 8)], corner.at[1, 0], 6, (down, gz_at(1))),
        remote(pack_low.at[:, pl.ds(0, 8)], corner.at[1, 1], 7, (down, gz_at(-1))),
    ]

    @pl.when(gy < ny - 1)
    def _():
        for copy in to_up:
            copy.start()

    @pl.when(gy > 0)
    def _():
        for copy in to_down:
            copy.start()

    for copy in copies:
        copy.start()

    load_weight.wait()
    root = jnp.sqrt(weight[...])
    row_i = lax.broadcasted_iota(jnp.int32, (width, width), 0)
    col_i = lax.broadcasted_iota(jnp.int32, (width, width), 1)
    j = row_i % 8
    position = jnp.where(j < 4, j - 4, width + j - 4)
    matrix = jnp.concatenate(
        [band(jnp.abs(row_i - col_i)) * root, band(jnp.abs(position - col_i)) * root], axis=0
    )
    matrix_high, matrix_low = split(matrix)
    matrix_both = jnp.concatenate([matrix_high, matrix_low], axis=1)

    @pl.when(gy > 0)
    def _():
        for copy in to_up:
            copy.wait_recv()

    @pl.when(gy < ny - 1)
    def _():
        for copy in to_down:
            copy.wait_recv()

    halo[:, pl.ds(0, 8), :] = jnp.where(
        left_lanes, lane_roll(corner[0, 0], width - 4), lane_roll(corner[1, 0], 4))
    halo[:, pl.ds(8, half), :] = jnp.where(left_lanes, side[0], side[1])
    halo[:, pl.ds(8 + half, half), :] = jnp.where(
        left_lanes, lane_roll(side[0], width - 4), lane_roll(side[1], 4))
    halo[:, pl.ds(8 + cells, 8), :] = jnp.where(left_lanes, corner[0, 1], corner[1, 1])
    halo_z = jnp.concatenate([filter_z(halo, c, cells) for c in range(comps)], axis=0)
    halo_high, halo_low = split(halo_z)

    for copy in copies:
        copy.wait_recv()

    def smooth_one(s, carry):
        field_z = jnp.concatenate(
            [filter_z(field, comps * s + c, cells) for c in range(comps)], axis=0)
        high, low = split(field_z)
        keep = (lane // 8 == s).astype(F32).astype(BF16)
        left = jnp.dot(
            jnp.concatenate([high, halo_high * keep], axis=1), matrix_both,
            preferred_element_type=F32)
        right = jnp.dot(
            jnp.concatenate([low, halo_low * keep], axis=1), matrix_high,
            preferred_element_type=F32)
        smooth = left[:, :width] + left[:, width:] + right
        high = smooth.astype(BF16)
        rest = smooth - high.astype(F32)
        low = rest.astype(BF16)
        square[s] = (rest * rest).reshape(-1, 8, width).sum(axis=0)
        for n in range(comps * cells // 16):
            rows_high[s, :, pl.ds(width * n, width)] = high[16 * n:16 * n + 16]
            rows_low[s, :, pl.ds(width * n, width)] = low[16 * n:16 * n + 16]
        return carry

    lax.fori_loop(0, snaps, smooth_one, 0)

    chunks = comps * cells // 16
    size = snaps * 16
    high = rows_high[...].reshape(size, width * chunks)
    low = rows_low[...].reshape(size, width * chunks)
    dims = (((1,), (1,)), ((), ()))
    big_i = lax.broadcasted_iota(jnp.int32, (size, size), 0)
    big_j = lax.broadcasted_iota(jnp.int32, (size, size), 1)
    same = big_i % 16 == big_j % 16

    def equal_z(left, right):
        big = lax.dot_general(left, right, dims, preferred_element_type=F32)
        return jnp.where(same, big, 0.0).reshape(snaps, 16, size).sum(axis=1)

    main, cross = equal_z(high, high), equal_z(low, high)
    groups = width // snaps
    gather_i = lax.broadcasted_iota(jnp.int32, (size, width), 0)
    gather_j = lax.broadcasted_iota(jnp.int32, (size, width), 1)
    gather = (gather_i // 16 == gather_j % snaps).astype(F32)
    other_i = lax.broadcasted_iota(jnp.int32, (snaps, size), 0)
    other_j = lax.broadcasted_iota(jnp.int32, (snaps, size), 1)
    other = (other_j // 16 == other_i).astype(F32)
    gram = jnp.dot(
        main + cross, gather, precision=lax.Precision.HIGHEST, preferred_element_type=F32)
    gram = gram + lax.dot_general(
        other, jnp.concatenate([cross] * groups, axis=0), dims,
        precision=lax.Precision.HIGHEST, preferred_element_type=F32)
    g_i = lax.broadcasted_iota(jnp.int32, (snaps, width), 0)
    g_j = lax.broadcasted_iota(jnp.int32, (snaps, width), 1)
    squares = jnp.sum(jnp.sum(square[...], axis=1), axis=1, keepdims=True)
    gram = gram + jnp.where(g_j % snaps == g_i, squares, 0.0)
    gram = jnp.where((g_j // snaps + g_i) % groups == 0, gram, 0.0)
    slots[mine] = gram.reshape(snaps // groups, groups, width).sum(axis=1)

    def share(step):
        return pltpu.make_async_remote_copy(
            src_ref=slots.at[mine], dst_ref=slots.at[mine],
            send_sem=gram_send.at[step], recv_sem=gram_recv.at[step],
            device_id=device_at(step), device_id_type=MESH,
        )

    def each(act):
        def body(step, carry):
            act(share(step))
            return carry
        lax.fori_loop(1, devices, body, 0, unroll=devices <= 64)

    each(lambda copy: copy.start())
    each(lambda copy: copy.wait_recv())
    gram_ref[...] = jnp.sum(slots[...], axis=0)

    each(lambda copy: copy.wait_send())
    for copy in copies:
        copy.wait_send()

    @pl.when(gy < ny - 1)
    def _():
        for copy in to_up:
            copy.wait_send()

    @pl.when(gy > 0)
    def _():
        for copy in to_down:
            copy.wait_send()


def modes_kernel(
    snaps, row_total, rows_high, rows_low, gram_ref, modes_ref, factor_ref,
    modes, factor, out_sem,
):
    width = gram_ref.shape[1]
    groups = width // snaps
    size = snaps * 16
    chunks = rows_high.shape[2] // width
    m_i = lax.broadcasted_iota(jnp.int32, (snaps, width), 0)
    m_j = lax.broadcasted_iota(jnp.int32, (snaps, width), 1)
    gram = jnp.concatenate([
        pltpu.roll(
            jnp.broadcast_to(gram_ref[n:n + 1, :], (groups, width)), 0, 1,
            stride=snaps, stride_axis=0)
        for n in range(snaps // groups)
    ], axis=0)
    gram = jnp.where(m_j < snaps, gram, 0.0)

    work = jnp.where(m_j == m_i + snaps, 1.0, gram)
    for k in range(snaps - 1):
        scaled = work[k:k + 1, :] / work[k:k + 1, k:k + 1]
        work = work - jnp.where(m_i > k, work[:, k:k + 1], 0.0) * scaled
    pivots = jnp.sum(jnp.where(m_i == m_j, work, 0.0), axis=1, keepdims=True)
    work = work / jnp.sqrt(pivots)
    upper = jnp.where(m_j >= m_i, work, 0.0) * (1.0 / math.sqrt(row_total))
    factor[...] = upper[:, :snaps]
    copies = [pltpu.make_async_copy(factor, factor_ref, out_sem.at[0])]
    copies[0].start()

    inverse_high, inverse_low = split(work * math.sqrt(row_total))
    spread_i = lax.broadcasted_iota(jnp.int32, (width, size), 0)
    spread_j = lax.broadcasted_iota(jnp.int32, (width, size), 1)
    spread = (spread_i - snaps == spread_j // 16).astype(F32).astype(BF16)

    same_i = lax.broadcasted_iota(jnp.int32, (size, size), 0)
    same_j = lax.broadcasted_iota(jnp.int32, (size, size), 1)
    same = same_i % 16 == same_j % 16

    def blocks(value):
        tall = jnp.broadcast_to(
            value.astype(F32)[:, None, :], (snaps, 16, width)).reshape(size, width).astype(BF16)
        wide = jnp.dot(tall, spread, preferred_element_type=F32)
        return jnp.where(same, wide, 0.0).astype(BF16)

    inverse_high, inverse_low = blocks(inverse_high), blocks(inverse_low)
    parts = out_sem.shape[0] - 1
    for q in range(parts):
        depth = chunks // parts
        for n in range(q * depth, (q + 1) * depth, 2):
            high = rows_high[:, :, pl.ds(width * n, 2 * width)].reshape(size, 2 * width)
            low = rows_low[:, :, pl.ds(width * n, 2 * width)].reshape(size, 2 * width)
            out = jnp.dot(inverse_high, high, preferred_element_type=F32)
            out = out + jnp.dot(inverse_high, low, preferred_element_type=F32)
            out = out + jnp.dot(inverse_low, high, preferred_element_type=F32)
            for m in range(2):
                modes[:, pl.ds(16 * (n + m), 16), :] = out[
                    :, m * width:(m + 1) * width].reshape(snaps, 16, width)
        span = pl.ds(16 * q * depth, 16 * depth)
        copies.append(pltpu.make_async_copy(
            modes.at[:, span], modes_ref.at[:, span], out_sem.at[q + 1]))
        copies[-1].start()
    for copy in copies:
        copy.wait()


def per_device(snapshots, cell_weight):
    snaps, comps, planes, cells, width = snapshots.shape
    comps_all = comps * planes
    ny, nz = lax.axis_size("gy"), lax.axis_size("gz")
    row_total = comps_all * cells * width * ny * nz
    devices = ny * nz
    depth = width * comps_all * cells // 16
    vmem = pl.BlockSpec(memory_space=pltpu.VMEM)
    hbm = pl.BlockSpec(memory_space=pltpu.HBM)
    rows_high, rows_low, gram = pl.pallas_call(
        functools.partial(rows_kernel, snaps, comps_all),
        out_shape=(
            jax.ShapeDtypeStruct((snaps, 16, depth), BF16),
            jax.ShapeDtypeStruct((snaps, 16, depth), BF16),
            jax.ShapeDtypeStruct((snaps * snaps // width, width), F32),
        ),
        in_specs=[hbm, hbm],
        out_specs=(vmem, vmem, vmem),
        scratch_shapes=[
            pltpu.VMEM((snaps * comps_all, cells + 16, width), F32),
            pltpu.VMEM((1, width), F32),
            pltpu.VMEM((comps_all, cells // 2, width), F32),
            pltpu.VMEM((comps_all, cells // 2, width), F32),
            pltpu.VMEM((2, comps_all, cells // 2, width), F32),
            pltpu.VMEM((2, 2, comps_all, 8, width), F32),
            pltpu.VMEM((comps_all, cells + 16, width), F32),
            pltpu.VMEM((snaps, 8, width), F32),
            pltpu.VMEM((devices, snaps * snaps // width, width), F32),
            pltpu.SemaphoreType.DMA((5,)),
            pltpu.SemaphoreType.DMA((8,)),
            pltpu.SemaphoreType.DMA((8,)),
            pltpu.SemaphoreType.DMA((devices,)),
            pltpu.SemaphoreType.DMA((devices,)),
        ],
        compiler_params=pltpu.CompilerParams(
            collective_id=0, has_side_effects=True, vmem_limit_bytes=32 * 1024 * 1024
        ),
    )(snapshots.reshape(snaps * comps_all, cells, width), cell_weight.reshape(1, width))
    modes, factor = pl.pallas_call(
        functools.partial(modes_kernel, snaps, row_total),
        out_shape=(
            jax.ShapeDtypeStruct((snaps, comps_all * cells, width), F32),
            jax.ShapeDtypeStruct((snaps, snaps), F32),
        ),
        in_specs=[vmem, vmem, vmem],
        out_specs=(hbm, hbm),
        scratch_shapes=[
            pltpu.VMEM((snaps, comps_all * cells, width), F32),
            pltpu.VMEM((snaps, snaps), F32),
            pltpu.SemaphoreType.DMA((4,)),
        ],
        compiler_params=pltpu.CompilerParams(vmem_limit_bytes=32 * 1024 * 1024),
    )(rows_high, rows_low, gram)
    return modes.reshape(snapshots.shape), factor


def solution(mesh):
    return jax.shard_map(
        per_device,
        mesh=mesh,
        in_specs=(P(None, None, None, "gz", "gy"), P("gy")),
        out_specs=(P(None, None, None, "gz", "gy"), P()),
        check_vma=False,
    )
```

```python
import functools
import math

import jax
import jax.numpy as jnp
from jax import lax
from jax.experimental import pallas as pl
from jax.experimental.pallas import tpu as pltpu
from jax.sharding import PartitionSpec as P

FILTER_RAW = [math.exp(-(offset - 4) * (offset - 4) / 4.5) for offset in range(9)]
FILTER_TAPS = [value / sum(FILTER_RAW) for value in FILTER_RAW]
HALF_TAPS = FILTER_TAPS[4:]

MESH = pl.DeviceIdType.MESH
F32, BF16 = jnp.float32, jnp.bfloat16


def split(value):
    high = value.astype(BF16)
    return high, (value - high.astype(F32)).astype(BF16)


def band(distance):
    out = jnp.zeros(distance.shape, F32)
    for k in range(5):
        out = jnp.where(distance == k, HALF_TAPS[k], out)
    return out


def lane_roll(value, shift):
    flat = value.reshape(-1, value.shape[-1])
    return pltpu.roll(flat, shift, 1).reshape(value.shape)


def filter_z(ref, index, cells):
    out = HALF_TAPS[0] * ref[index, pl.ds(8, cells), :]
    for k in range(1, 5):
        out = out + HALF_TAPS[k] * (
            ref[index, pl.ds(8 - k, cells), :] + ref[index, pl.ds(8 + k, cells), :]
        )
    return out


def rows_kernel(
    snaps, comps, x_ref, w_ref, high_ref, low_ref, gram_ref,
    field, rows_high, rows_low, weight, pack_low, pack_high, side, corner, halo, square, slots,
    load_sem, store_sem, halo_send, halo_recv, gram_send, gram_recv,
):
    cells, width = x_ref.shape[1], x_ref.shape[2]
    half = cells // 2
    gy, gz = lax.axis_index("gy"), lax.axis_index("gz")
    ny, nz = lax.axis_size("gy"), lax.axis_size("gz")

    def gz_at(step):
        return lax.rem(gz + step + nz, nz)

    loads = []
    part = snaps * comps // 4
    for q in range(4):
        loads.append(pltpu.make_async_copy(
            x_ref.at[pl.ds(q * part, part)],
            field.at[pl.ds(q * part, part), pl.ds(8, cells)],
            load_sem.at[q],
        ))
        loads[-1].start()
    load_weight = pltpu.make_async_copy(w_ref, weight, load_sem.at[4])
    load_weight.start()
    side[...] = jnp.zeros_like(side)
    corner[...] = jnp.zeros_like(corner)

    barrier = pltpu.get_barrier_semaphore()
    devices = ny * nz
    mine = gy * nz + gz

    def device_at(step):
        flat = lax.rem(mine + step, devices)
        return flat // nz, lax.rem(flat, nz)

    def greet(step, carry):
        pl.semaphore_signal(barrier, inc=1, device_id=device_at(step), device_id_type=MESH)
        return carry

    lax.fori_loop(1, devices, greet, 0, unroll=devices <= 64)

    lane = lax.broadcasted_iota(jnp.int32, (1, width), 1)
    packed = jnp.zeros((comps * cells, width), F32)
    for s in range(snaps):
        if s % 4 == 0:
            loads[s // 4].wait()
        block = field[pl.ds(comps * s, comps), pl.ds(8, cells), :].reshape(comps * cells, width)
        packed = jnp.where(lane // 8 == s, pltpu.roll(block, (4 + 8 * s) % width, 1), packed)
    packed = packed.reshape(comps, cells, width)
    first, second = packed[:, :half], packed[:, half:]
    left_lanes = (lane % 8 < 4).reshape(1, 1, width)
    pack_high[...] = jnp.where(left_lanes, first, lane_roll(second, 4))
    pack_low[...] = jnp.where(left_lanes, lane_roll(second, width - 4), first)

    pl.semaphore_wait(barrier, devices - 1)

    def remote(src, dst, n, target):
        return pltpu.make_async_remote_copy(
            src_ref=src, dst_ref=dst, send_sem=halo_send.at[n], recv_sem=halo_recv.at[n],
            device_id=target, device_id_type=MESH,
        )

    copies = [
        remote(x_ref.at[:, pl.ds(cells - 4, 4), :], field.at[:, pl.ds(4, 4), :], 0, (gy, gz_at(1))),
        remote(x_ref.at[:, pl.ds(0, 4), :], field.at[:, pl.ds(cells + 8, 4), :], 1, (gy, gz_at(-1))),
    ]
    up = jnp.minimum(gy + 1, ny - 1)
    down = jnp.maximum(gy - 1, 0)
    to_up = [
        remote(pack_high, side.at[0], 2, (up, gz)),
        remote(pack_high.at[:, pl.ds(half - 8, 8)], corner.at[0, 0], 3, (up, gz_at(1))),
        remote(pack_high.at[:, pl.ds(0, 8)], corner.at[0, 1], 4, (up, gz_at(-1))),
    ]
    to_down = [
        remote(pack_low, side.at[1], 5, (down, gz)),
        remote(pack_low.at[:, pl.ds(half - 8, 8)], corner.at[1, 0], 6, (down, gz_at(1))),
        remote(pack_low.at[:, pl.ds(0, 8)], corner.at[1, 1], 7, (down, gz_at(-1))),
    ]

    @pl.when(gy < ny - 1)
    def _():
        for copy in to_up:
            copy.start()

    @pl.when(gy > 0)
    def _():
        for copy in to_down:
            copy.start()

    for copy in copies:
        copy.start()

    load_weight.wait()
    root = jnp.sqrt(weight[...])
    row_i = lax.broadcasted_iota(jnp.int32, (width, width), 0)
    col_i = lax.broadcasted_iota(jnp.int32, (width, width), 1)
    j = row_i % 8
    position = jnp.where(j < 4, j - 4, width + j - 4)
    matrix = jnp.concatenate(
        [band(jnp.abs(row_i - col_i)) * root, band(jnp.abs(position - col_i)) * root], axis=0
    )
    matrix_high, matrix_low = split(matrix)
    matrix_both = jnp.concatenate([matrix_high, matrix_low], axis=1)

    @pl.when(gy > 0)
    def _():
        for copy in to_up:
            copy.wait_recv()

    @pl.when(gy < ny - 1)
    def _():
        for copy in to_down:
            copy.wait_recv()

    halo[:, pl.ds(0, 8), :] = jnp.where(
        left_lanes, lane_roll(corner[0, 0], width - 4), lane_roll(corner[1, 0], 4))
    halo[:, pl.ds(8, half), :] = jnp.where(left_lanes, side[0], side[1])
    halo[:, pl.ds(8 + half, half), :] = jnp.where(
        left_lanes, lane_roll(side[0], width - 4), lane_roll(side[1], 4))
    halo[:, pl.ds(8 + cells, 8), :] = jnp.where(left_lanes, corner[0, 1], corner[1, 1])
    halo_z = jnp.concatenate([filter_z(halo, c, cells) for c in range(comps)], axis=0)
    halo_high, halo_low = split(halo_z)

    for copy in copies:
        copy.wait_recv()

    def smooth_one(s, carry):
        field_z = jnp.concatenate(
            [filter_z(field, comps * s + c, cells) for c in range(comps)], axis=0)
        high, low = split(field_z)
        keep = (lane // 8 == s).astype(F32).astype(BF16)
        left = jnp.dot(
            jnp.concatenate([high, halo_high * keep], axis=1), matrix_both,
            preferred_element_type=F32)
        right = jnp.dot(
            jnp.concatenate([low, halo_low * keep], axis=1), matrix_high,
            preferred_element_type=F32)
        smooth = left[:, :width] + left[:, width:] + right
        high = smooth.astype(BF16)
        rest = smooth - high.astype(F32)
        low = rest.astype(BF16)
        square[s] = (rest * rest).reshape(-1, 8, width).sum(axis=0)
        for n in range(comps * cells // 16):
            rows_high[s, :, pl.ds(width * n, width)] = high[16 * n:16 * n + 16]
            rows_low[s, :, pl.ds(width * n, width)] = low[16 * n:16 * n + 16]
        return carry

    lax.fori_loop(0, snaps, smooth_one, 0)

    stores = [
        pltpu.make_async_copy(rows_high, high_ref, store_sem.at[0]),
        pltpu.make_async_copy(rows_low, low_ref, store_sem.at[1]),
    ]
    for store in stores:
        store.start()

    chunks = comps * cells // 16
    size = snaps * 16
    high = rows_high[...].reshape(size, width * chunks)
    low = rows_low[...].reshape(size, width * chunks)
    dims = (((1,), (1,)), ((), ()))
    big_i = lax.broadcasted_iota(jnp.int32, (size, size), 0)
    big_j = lax.broadcasted_iota(jnp.int32, (size, size), 1)
    same = big_i % 16 == big_j % 16

    def equal_z(left, right):
        big = lax.dot_general(left, right, dims, preferred_element_type=F32)
        return jnp.where(same, big, 0.0).reshape(snaps, 16, size).sum(axis=1)

    main, cross = equal_z(high, high), equal_z(low, high)
    groups = width // snaps
    gather_i = lax.broadcasted_iota(jnp.int32, (size, width), 0)
    gather_j = lax.broadcasted_iota(jnp.int32, (size, width), 1)
    gather = (gather_i // 16 == gather_j % snaps).astype(F32)
    other_i = lax.broadcasted_iota(jnp.int32, (snaps, size), 0)
    other_j = lax.broadcasted_iota(jnp.int32, (snaps, size), 1)
    other = (other_j // 16 == other_i).astype(F32)
    gram = jnp.dot(
        main + cross, gather, precision=lax.Precision.HIGHEST, preferred_element_type=F32)
    gram = gram + lax.dot_general(
        other, jnp.concatenate([cross] * groups, axis=0), dims,
        precision=lax.Precision.HIGHEST, preferred_element_type=F32)
    g_i = lax.broadcasted_iota(jnp.int32, (snaps, width), 0)
    g_j = lax.broadcasted_iota(jnp.int32, (snaps, width), 1)
    squares = jnp.sum(jnp.sum(square[...], axis=1), axis=1, keepdims=True)
    gram = gram + jnp.where(g_j % snaps == g_i, squares, 0.0)
    gram = jnp.where((g_j // snaps + g_i) % groups == 0, gram, 0.0)
    slots[mine] = gram.reshape(snaps // groups, groups, width).sum(axis=1)

    def share(step):
        return pltpu.make_async_remote_copy(
            src_ref=slots.at[mine], dst_ref=slots.at[mine],
            send_sem=gram_send.at[step], recv_sem=gram_recv.at[step],
            device_id=device_at(step), device_id_type=MESH,
        )

    def each(act):
        def body(step, carry):
            act(share(step))
            return carry
        lax.fori_loop(1, devices, body, 0, unroll=devices <= 64)

    each(lambda copy: copy.start())
    each(lambda copy: copy.wait_recv())
    gram_ref[...] = jnp.sum(slots[...], axis=0)

    for store in stores:
        store.wait()
    each(lambda copy: copy.wait_send())
    for copy in copies:
        copy.wait_send()

    @pl.when(gy < ny - 1)
    def _():
        for copy in to_up:
            copy.wait_send()

    @pl.when(gy > 0)
    def _():
        for copy in to_down:
            copy.wait_send()


def modes_kernel(
    snaps, row_total, high_ref, low_ref, gram_ref, modes_ref, factor_ref,
    rows_high, rows_low, modes, factor, load_sem, out_sem,
):
    loads = [
        pltpu.make_async_copy(high_ref, rows_high, load_sem.at[0]),
        pltpu.make_async_copy(low_ref, rows_low, load_sem.at[1]),
    ]
    for load in loads:
        load.start()
    width = gram_ref.shape[1]
    groups = width // snaps
    size = snaps * 16
    chunks = rows_high.shape[2] // width
    m_i = lax.broadcasted_iota(jnp.int32, (snaps, width), 0)
    m_j = lax.broadcasted_iota(jnp.int32, (snaps, width), 1)
    gram = jnp.concatenate([
        pltpu.roll(
            jnp.broadcast_to(gram_ref[n:n + 1, :], (groups, width)), 0, 1,
            stride=snaps, stride_axis=0)
        for n in range(snaps // groups)
    ], axis=0)
    gram = jnp.where(m_j < snaps, gram, 0.0)

    work = jnp.where(m_j == m_i + snaps, 1.0, gram)
    for k in range(snaps - 1):
        scaled = work[k:k + 1, :] / work[k:k + 1, k:k + 1]
        work = work - jnp.where(m_i > k, work[:, k:k + 1], 0.0) * scaled
    pivots = jnp.sum(jnp.where(m_i == m_j, work, 0.0), axis=1, keepdims=True)
    work = work / jnp.sqrt(pivots)
    upper = jnp.where(m_j >= m_i, work, 0.0) * (1.0 / math.sqrt(row_total))
    factor[...] = upper[:, :snaps]
    copies = [pltpu.make_async_copy(factor, factor_ref, out_sem.at[0])]
    copies[0].start()

    inverse_high, inverse_low = split(work * math.sqrt(row_total))
    spread_i = lax.broadcasted_iota(jnp.int32, (width, size), 0)
    spread_j = lax.broadcasted_iota(jnp.int32, (width, size), 1)
    spread = (spread_i - snaps == spread_j // 16).astype(F32).astype(BF16)

    same_i = lax.broadcasted_iota(jnp.int32, (size, size), 0)
    same_j = lax.broadcasted_iota(jnp.int32, (size, size), 1)
    same = same_i % 16 == same_j % 16

    def blocks(value):
        tall = jnp.broadcast_to(
            value.astype(F32)[:, None, :], (snaps, 16, width)).reshape(size, width).astype(BF16)
        wide = jnp.dot(tall, spread, preferred_element_type=F32)
        return jnp.where(same, wide, 0.0).astype(BF16)

    inverse_high, inverse_low = blocks(inverse_high), blocks(inverse_low)
    for load in loads:
        load.wait()
    parts = out_sem.shape[0] - 1
    for q in range(parts):
        depth = chunks // parts
        for n in range(q * depth, (q + 1) * depth, 2):
            high = rows_high[:, :, pl.ds(width * n, 2 * width)].reshape(size, 2 * width)
            low = rows_low[:, :, pl.ds(width * n, 2 * width)].reshape(size, 2 * width)
            out = jnp.dot(inverse_high, high, preferred_element_type=F32)
            out = out + jnp.dot(inverse_high, low, preferred_element_type=F32)
            out = out + jnp.dot(inverse_low, high, preferred_element_type=F32)
            for m in range(2):
                modes[:, pl.ds(16 * (n + m), 16), :] = out[
                    :, m * width:(m + 1) * width].reshape(snaps, 16, width)
        span = pl.ds(16 * q * depth, 16 * depth)
        copies.append(pltpu.make_async_copy(
            modes.at[:, span], modes_ref.at[:, span], out_sem.at[q + 1]))
        copies[-1].start()
    for copy in copies:
        copy.wait()


def per_device(snapshots, cell_weight):
    snaps, comps, planes, cells, width = snapshots.shape
    comps_all = comps * planes
    ny, nz = lax.axis_size("gy"), lax.axis_size("gz")
    row_total = comps_all * cells * width * ny * nz
    devices = ny * nz
    depth = width * comps_all * cells // 16
    vmem = pl.BlockSpec(memory_space=pltpu.VMEM)
    hbm = pl.BlockSpec(memory_space=pltpu.HBM)
    rows_high, rows_low, gram = pl.pallas_call(
        functools.partial(rows_kernel, snaps, comps_all),
        out_shape=(
            jax.ShapeDtypeStruct((snaps, 16, depth), BF16),
            jax.ShapeDtypeStruct((snaps, 16, depth), BF16),
            jax.ShapeDtypeStruct((snaps * snaps // width, width), F32),
        ),
        in_specs=[hbm, hbm],
        out_specs=(hbm, hbm, vmem),
        scratch_shapes=[
            pltpu.VMEM((snaps * comps_all, cells + 16, width), F32),
            pltpu.VMEM((snaps, 16, depth), BF16),
            pltpu.VMEM((snaps, 16, depth), BF16),
            pltpu.VMEM((1, width), F32),
            pltpu.VMEM((comps_all, cells // 2, width), F32),
            pltpu.VMEM((comps_all, cells // 2, width), F32),
            pltpu.VMEM((2, comps_all, cells // 2, width), F32),
            pltpu.VMEM((2, 2, comps_all, 8, width), F32),
            pltpu.VMEM((comps_all, cells + 16, width), F32),
            pltpu.VMEM((snaps, 8, width), F32),
            pltpu.VMEM((devices, snaps * snaps // width, width), F32),
            pltpu.SemaphoreType.DMA((5,)),
            pltpu.SemaphoreType.DMA((2,)),
            pltpu.SemaphoreType.DMA((8,)),
            pltpu.SemaphoreType.DMA((8,)),
            pltpu.SemaphoreType.DMA((devices,)),
            pltpu.SemaphoreType.DMA((devices,)),
        ],
        compiler_params=pltpu.CompilerParams(
            collective_id=0, has_side_effects=True, vmem_limit_bytes=60 * 1024 * 1024
        ),
    )(snapshots.reshape(snaps * comps_all, cells, width), cell_weight.reshape(1, width))
    modes, factor = pl.pallas_call(
        functools.partial(modes_kernel, snaps, row_total),
        out_shape=(
            jax.ShapeDtypeStruct((snaps, comps_all * cells, width), F32),
            jax.ShapeDtypeStruct((snaps, snaps), F32),
        ),
        in_specs=[hbm, hbm, vmem],
        out_specs=(hbm, hbm),
        scratch_shapes=[
            pltpu.VMEM((snaps, 16, depth), BF16),
            pltpu.VMEM((snaps, 16, depth), BF16),
            pltpu.VMEM((snaps, comps_all * cells, width), F32),
            pltpu.VMEM((snaps, snaps), F32),
            pltpu.SemaphoreType.DMA((2,)),
            pltpu.SemaphoreType.DMA((4,)),
        ],
        compiler_params=pltpu.CompilerParams(vmem_limit_bytes=60 * 1024 * 1024),
    )(rows_high, rows_low, gram)
    return modes.reshape(snapshots.shape), factor


def solution(mesh):
    return jax.shard_map(
        per_device,
        mesh=mesh,
        in_specs=(P(None, None, None, "gz", "gy"), P("gy")),
        out_specs=(P(None, None, None, "gz", "gy"), P()),
        check_vma=False,
    )
```

```python
import functools
import math

import jax
import jax.numpy as jnp
from jax import lax
from jax.experimental import pallas as pl
from jax.experimental.pallas import tpu as pltpu
from jax.sharding import PartitionSpec as P

FILTER_RAW = [math.exp(-(offset - 4) * (offset - 4) / 4.5) for offset in range(9)]
FILTER_TAPS = [value / sum(FILTER_RAW) for value in FILTER_RAW]
HALF_TAPS = FILTER_TAPS[4:]

MESH = pl.DeviceIdType.MESH
F32, BF16 = jnp.float32, jnp.bfloat16


def split(value):
    high = value.astype(BF16)
    return high, (value - high.astype(F32)).astype(BF16)


def band(distance):
    out = jnp.zeros(distance.shape, F32)
    for k in range(5):
        out = jnp.where(distance == k, HALF_TAPS[k], out)
    return out


def lane_roll(value, shift):
    flat = value.reshape(-1, value.shape[-1])
    return pltpu.roll(flat, shift, 1).reshape(value.shape)


def filter_z(ref, index, start, cells):
    out = HALF_TAPS[0] * ref[index, pl.ds(8 + start, cells), :]
    for k in range(1, 5):
        out = out + HALF_TAPS[k] * (
            ref[index, pl.ds(8 + start - k, cells), :] + ref[index, pl.ds(8 + start + k, cells), :]
        )
    return out


def product(high, low, both, width):
    out = jnp.dot(high, both, preferred_element_type=F32)
    return out[:, :width] + out[:, width:] + jnp.dot(
        low, both[:, :width], preferred_element_type=F32)


def rows_kernel(
    snaps, comps, x_ref, w_ref, high_ref, low_ref, gram_ref,
    field, rows_high, rows_low, inner, weight, pack_low, pack_high, side, corner, halo, square, slots,
    load_sem, store_sem, halo_send, halo_recv, gram_send, gram_recv,
):
    cells, width = x_ref.shape[1], x_ref.shape[2]
    half = cells // 2
    gy, gz = lax.axis_index("gy"), lax.axis_index("gz")
    ny, nz = lax.axis_size("gy"), lax.axis_size("gz")

    def gz_at(step):
        return lax.rem(gz + step + nz, nz)

    loads = []
    part = snaps * comps // 4
    for q in range(4):
        loads.append(pltpu.make_async_copy(
            x_ref.at[pl.ds(q * part, part)],
            field.at[pl.ds(q * part, part), pl.ds(8, cells)],
            load_sem.at[q],
        ))
        loads[-1].start()
    load_weight = pltpu.make_async_copy(w_ref, weight, load_sem.at[4])
    load_weight.start()
    side[...] = jnp.zeros_like(side)
    corner[...] = jnp.zeros_like(corner)

    barrier = pltpu.get_barrier_semaphore()
    devices = ny * nz
    mine = gy * nz + gz

    def device_at(step):
        flat = lax.rem(mine + step, devices)
        return flat // nz, lax.rem(flat, nz)

    def greet(step, carry):
        pl.semaphore_signal(barrier, inc=1, device_id=device_at(step), device_id_type=MESH)
        return carry

    lax.fori_loop(1, devices, greet, 0, unroll=devices <= 64)

    lane = lax.broadcasted_iota(jnp.int32, (1, width), 1)
    packed = jnp.zeros((comps * cells, width), F32)
    for s in range(snaps):
        if s % 4 == 0:
            loads[s // 4].wait()
        block = field[pl.ds(comps * s, comps), pl.ds(8, cells), :].reshape(comps * cells, width)
        packed = jnp.where(lane // 8 == s, pltpu.roll(block, (4 + 8 * s) % width, 1), packed)
    packed = packed.reshape(comps, cells, width)
    first, second = packed[:, :half], packed[:, half:]
    left_lanes = (lane % 8 < 4).reshape(1, 1, width)
    pack_high[...] = jnp.where(left_lanes, first, lane_roll(second, 4))
    pack_low[...] = jnp.where(left_lanes, lane_roll(second, width - 4), first)

    pl.semaphore_wait(barrier, devices - 1)

    def remote(src, dst, n, target):
        return pltpu.make_async_remote_copy(
            src_ref=src, dst_ref=dst, send_sem=halo_send.at[n], recv_sem=halo_recv.at[n],
            device_id=target, device_id_type=MESH,
        )

    copies = [
        remote(x_ref.at[:, pl.ds(cells - 4, 4), :], field.at[:, pl.ds(4, 4), :], 0, (gy, gz_at(1))),
        remote(x_ref.at[:, pl.ds(0, 4), :], field.at[:, pl.ds(cells + 8, 4), :], 1, (gy, gz_at(-1))),
    ]
    up = jnp.minimum(gy + 1, ny - 1)
    down = jnp.maximum(gy - 1, 0)
    to_up = [
        remote(pack_high, side.at[0], 2, (up, gz)),
        remote(pack_high.at[:, pl.ds(half - 8, 8)], corner.at[0, 0], 3, (up, gz_at(1))),
        remote(pack_high.at[:, pl.ds(0, 8)], corner.at[0, 1], 4, (up, gz_at(-1))),
    ]
    to_down = [
        remote(pack_low, side.at[1], 5, (down, gz)),
        remote(pack_low.at[:, pl.ds(half - 8, 8)], corner.at[1, 0], 6, (down, gz_at(1))),
        remote(pack_low.at[:, pl.ds(0, 8)], corner.at[1, 1], 7, (down, gz_at(-1))),
    ]

    @pl.when(gy < ny - 1)
    def _():
        for copy in to_up:
            copy.start()

    @pl.when(gy > 0)
    def _():
        for copy in to_down:
            copy.start()

    for copy in copies:
        copy.start()

    load_weight.wait()
    root = jnp.sqrt(weight[...])
    row_i = lax.broadcasted_iota(jnp.int32, (width, width), 0)
    col_i = lax.broadcasted_iota(jnp.int32, (width, width), 1)
    j = row_i % 8
    position = jnp.where(j < 4, j - 4, width + j - 4)
    own_both = jnp.concatenate(split(band(jnp.abs(row_i - col_i)) * root), axis=1)
    halo_both = jnp.concatenate(split(band(jnp.abs(position - col_i)) * root), axis=1)

    deep = cells - 16

    def smooth_inner(s, carry):
        high, low = split(jnp.concatenate(
            [filter_z(field, comps * s + c, 8, deep) for c in range(comps)], axis=0))
        inner[s] = product(high, low, own_both, width)
        return carry

    lax.fori_loop(0, snaps, smooth_inner, 0, unroll=True)

    @pl.when(gy > 0)
    def _():
        for copy in to_up:
            copy.wait_recv()

    @pl.when(gy < ny - 1)
    def _():
        for copy in to_down:
            copy.wait_recv()

    halo[:, pl.ds(0, 8), :] = jnp.where(
        left_lanes, lane_roll(corner[0, 0], width - 4), lane_roll(corner[1, 0], 4))
    halo[:, pl.ds(8, half), :] = jnp.where(left_lanes, side[0], side[1])
    halo[:, pl.ds(8 + half, half), :] = jnp.where(
        left_lanes, lane_roll(side[0], width - 4), lane_roll(side[1], 4))
    halo[:, pl.ds(8 + cells, 8), :] = jnp.where(left_lanes, corner[0, 1], corner[1, 1])
    halo_z = jnp.concatenate([filter_z(halo, c, 0, cells) for c in range(comps)], axis=0)
    halo_high, halo_low = split(halo_z)

    for copy in copies:
        copy.wait_recv()

    def smooth_one(s, carry):
        high, low = split(jnp.concatenate(
            [filter_z(field, comps * s + c, z, 8) for c in range(comps) for z in (0, cells - 8)],
            axis=0))
        edge = product(high, low, own_both, width)
        keep = (lane // 8 == s).astype(F32).astype(BF16)
        smooth = product(halo_high * keep, halo_low * keep, halo_both, width)
        own = []
        for c in range(comps):
            own += [
                edge[16 * c:16 * c + 8], inner[s, pl.ds(deep * c, deep), :],
                edge[16 * c + 8:16 * c + 16],
            ]
        smooth = smooth + jnp.concatenate(own, axis=0)
        high = smooth.astype(BF16)
        rest = smooth - high.astype(F32)
        low = rest.astype(BF16)
        square[s] = (rest * rest).reshape(-1, 8, width).sum(axis=0)
        for n in range(comps * cells // 16):
            rows_high[s, :, pl.ds(width * n, width)] = high[16 * n:16 * n + 16]
            rows_low[s, :, pl.ds(width * n, width)] = low[16 * n:16 * n + 16]
        return carry

    lax.fori_loop(0, snaps, smooth_one, 0, unroll=True)

    stores = [
        pltpu.make_async_copy(rows_high, high_ref, store_sem.at[0]),
        pltpu.make_async_copy(rows_low, low_ref, store_sem.at[1]),
    ]
    for store in stores:
        store.start()

    chunks = comps * cells // 16
    size = snaps * 16
    high = rows_high[...].reshape(size, width * chunks)
    low = rows_low[...].reshape(size, width * chunks)
    dims = (((1,), (1,)), ((), ()))
    big_i = lax.broadcasted_iota(jnp.int32, (size, size), 0)
    big_j = lax.broadcasted_iota(jnp.int32, (size, size), 1)
    same = big_i % 16 == big_j % 16

    def equal_z(left, right):
        big = lax.dot_general(left, right, dims, preferred_element_type=F32)
        return jnp.where(same, big, 0.0).reshape(snaps, 16, size).sum(axis=1)

    main, cross = equal_z(high, high), equal_z(low, high)
    groups = width // snaps
    gather_i = lax.broadcasted_iota(jnp.int32, (size, width), 0)
    gather_j = lax.broadcasted_iota(jnp.int32, (size, width), 1)
    gather = (gather_i // 16 == gather_j % snaps).astype(F32)
    other_i = lax.broadcasted_iota(jnp.int32, (snaps, size), 0)
    other_j = lax.broadcasted_iota(jnp.int32, (snaps, size), 1)
    other = (other_j // 16 == other_i).astype(F32)
    gram = jnp.dot(
        main + cross, gather, precision=lax.Precision.HIGHEST, preferred_element_type=F32)
    gram = gram + lax.dot_general(
        other, jnp.concatenate([cross] * groups, axis=0), dims,
        precision=lax.Precision.HIGHEST, preferred_element_type=F32)
    g_i = lax.broadcasted_iota(jnp.int32, (snaps, width), 0)
    g_j = lax.broadcasted_iota(jnp.int32, (snaps, width), 1)
    squares = jnp.sum(jnp.sum(square[...], axis=1), axis=1, keepdims=True)
    gram = gram + jnp.where(g_j % snaps == g_i, squares, 0.0)
    gram = jnp.where((g_j // snaps + g_i) % groups == 0, gram, 0.0)
    slots[mine] = gram.reshape(snaps // groups, groups, width).sum(axis=1)

    def share(step):
        return pltpu.make_async_remote_copy(
            src_ref=slots.at[mine], dst_ref=slots.at[mine],
            send_sem=gram_send.at[step], recv_sem=gram_recv.at[step],
            device_id=device_at(step), device_id_type=MESH,
        )

    def each(act):
        def body(step, carry):
            act(share(step))
            return carry
        lax.fori_loop(1, devices, body, 0, unroll=devices <= 64)

    each(lambda copy: copy.start())
    each(lambda copy: copy.wait_recv())
    gram_ref[...] = jnp.sum(slots[...], axis=0)

    for store in stores:
        store.wait()
    each(lambda copy: copy.wait_send())
    for copy in copies:
        copy.wait_send()

    @pl.when(gy < ny - 1)
    def _():
        for copy in to_up:
            copy.wait_send()

    @pl.when(gy > 0)
    def _():
        for copy in to_down:
            copy.wait_send()


def modes_kernel(
    snaps, row_total, high_ref, low_ref, gram_ref, modes_ref, factor_ref,
    rows_high, rows_low, modes, factor, load_sem, out_sem,
):
    loads = [
        pltpu.make_async_copy(high_ref, rows_high, load_sem.at[0]),
        pltpu.make_async_copy(low_ref, rows_low, load_sem.at[1]),
    ]
    for load in loads:
        load.start()
    width = gram_ref.shape[1]
    groups = width // snaps
    size = snaps * 16
    chunks = rows_high.shape[2] // width
    m_i = lax.broadcasted_iota(jnp.int32, (snaps, width), 0)
    m_j = lax.broadcasted_iota(jnp.int32, (snaps, width), 1)
    gram = jnp.concatenate([
        pltpu.roll(
            jnp.broadcast_to(gram_ref[n:n + 1, :], (groups, width)), 0, 1,
            stride=snaps, stride_axis=0)
        for n in range(snaps // groups)
    ], axis=0)
    gram = jnp.where(m_j < snaps, gram, 0.0)

    work = jnp.where(m_j == m_i + snaps, 1.0, gram)
    for k in range(snaps - 1):
        scaled = work[k:k + 1, :] / work[k:k + 1, k:k + 1]
        work = work - jnp.where(m_i > k, work[:, k:k + 1], 0.0) * scaled
    pivots = jnp.sum(jnp.where(m_i == m_j, work, 0.0), axis=1, keepdims=True)
    work = work / jnp.sqrt(pivots)
    upper = jnp.where(m_j >= m_i, work, 0.0) * (1.0 / math.sqrt(row_total))
    factor[...] = upper[:, :snaps]
    copies = [pltpu.make_async_copy(factor, factor_ref, out_sem.at[0])]
    copies[0].start()

    inverse_high, inverse_low = split(work * math.sqrt(row_total))
    spread_i = lax.broadcasted_iota(jnp.int32, (width, size), 0)
    spread_j = lax.broadcasted_iota(jnp.int32, (width, size), 1)
    spread = (spread_i - snaps == spread_j // 16).astype(F32).astype(BF16)

    same_i = lax.broadcasted_iota(jnp.int32, (size, size), 0)
    same_j = lax.broadcasted_iota(jnp.int32, (size, size), 1)
    same = same_i % 16 == same_j % 16

    def blocks(value):
        tall = jnp.broadcast_to(
            value.astype(F32)[:, None, :], (snaps, 16, width)).reshape(size, width).astype(BF16)
        wide = jnp.dot(tall, spread, preferred_element_type=F32)
        return jnp.where(same, wide, 0.0).astype(BF16)

    inverse_high, inverse_low = blocks(inverse_high), blocks(inverse_low)
    for load in loads:
        load.wait()
    parts = out_sem.shape[0] - 1
    for q in range(parts):
        depth = chunks // parts
        for n in range(q * depth, (q + 1) * depth, 2):
            high = rows_high[:, :, pl.ds(width * n, 2 * width)].reshape(size, 2 * width)
            low = rows_low[:, :, pl.ds(width * n, 2 * width)].reshape(size, 2 * width)
            out = jnp.dot(inverse_high, high, preferred_element_type=F32)
            out = out + jnp.dot(inverse_high, low, preferred_element_type=F32)
            out = out + jnp.dot(inverse_low, high, preferred_element_type=F32)
            for m in range(2):
                modes[:, pl.ds(16 * (n + m), 16), :] = out[
                    :, m * width:(m + 1) * width].reshape(snaps, 16, width)
        span = pl.ds(16 * q * depth, 16 * depth)
        copies.append(pltpu.make_async_copy(
            modes.at[:, span], modes_ref.at[:, span], out_sem.at[q + 1]))
        copies[-1].start()
    for copy in copies:
        copy.wait()


def per_device(snapshots, cell_weight):
    snaps, comps, planes, cells, width = snapshots.shape
    comps_all = comps * planes
    ny, nz = lax.axis_size("gy"), lax.axis_size("gz")
    row_total = comps_all * cells * width * ny * nz
    devices = ny * nz
    depth = width * comps_all * cells // 16
    vmem = pl.BlockSpec(memory_space=pltpu.VMEM)
    hbm = pl.BlockSpec(memory_space=pltpu.HBM)
    rows_high, rows_low, gram = pl.pallas_call(
        functools.partial(rows_kernel, snaps, comps_all),
        out_shape=(
            jax.ShapeDtypeStruct((snaps, 16, depth), BF16),
            jax.ShapeDtypeStruct((snaps, 16, depth), BF16),
            jax.ShapeDtypeStruct((snaps * snaps // width, width), F32),
        ),
        in_specs=[hbm, hbm],
        out_specs=(hbm, hbm, vmem),
        scratch_shapes=[
            pltpu.VMEM((snaps * comps_all, cells + 16, width), F32),
            pltpu.VMEM((snaps, 16, depth), BF16),
            pltpu.VMEM((snaps, 16, depth), BF16),
            pltpu.VMEM((snaps, comps_all * (cells - 16), width), F32),
            pltpu.VMEM((1, width), F32),
            pltpu.VMEM((comps_all, cells // 2, width), F32),
            pltpu.VMEM((comps_all, cells // 2, width), F32),
            pltpu.VMEM((2, comps_all, cells // 2, width), F32),
            pltpu.VMEM((2, 2, comps_all, 8, width), F32),
            pltpu.VMEM((comps_all, cells + 16, width), F32),
            pltpu.VMEM((snaps, 8, width), F32),
            pltpu.VMEM((devices, snaps * snaps // width, width), F32),
            pltpu.SemaphoreType.DMA((5,)),
            pltpu.SemaphoreType.DMA((2,)),
            pltpu.SemaphoreType.DMA((8,)),
            pltpu.SemaphoreType.DMA((8,)),
            pltpu.SemaphoreType.DMA((devices,)),
            pltpu.SemaphoreType.DMA((devices,)),
        ],
        compiler_params=pltpu.CompilerParams(
            collective_id=0, has_side_effects=True, vmem_limit_bytes=60 * 1024 * 1024
        ),
    )(snapshots.reshape(snaps * comps_all, cells, width), cell_weight.reshape(1, width))
    modes, factor = pl.pallas_call(
        functools.partial(modes_kernel, snaps, row_total),
        out_shape=(
            jax.ShapeDtypeStruct((snaps, comps_all * cells, width), F32),
            jax.ShapeDtypeStruct((snaps, snaps), F32),
        ),
        in_specs=[hbm, hbm, vmem],
        out_specs=(hbm, hbm),
        scratch_shapes=[
            pltpu.VMEM((snaps, 16, depth), BF16),
            pltpu.VMEM((snaps, 16, depth), BF16),
            pltpu.VMEM((snaps, comps_all * cells, width), F32),
            pltpu.VMEM((snaps, snaps), F32),
            pltpu.SemaphoreType.DMA((2,)),
            pltpu.SemaphoreType.DMA((4,)),
        ],
        compiler_params=pltpu.CompilerParams(vmem_limit_bytes=60 * 1024 * 1024),
    )(rows_high, rows_low, gram)
    return modes.reshape(snapshots.shape), factor


def solution(mesh):
    return jax.shard_map(
        per_device,
        mesh=mesh,
        in_specs=(P(None, None, None, "gz", "gy"), P("gy")),
        out_specs=(P(None, None, None, "gz", "gy"), P()),
        check_vma=False,
    )
```

```python
import functools
import math

import jax
import jax.numpy as jnp
from jax import lax
from jax.experimental import pallas as pl
from jax.experimental.pallas import tpu as pltpu
from jax.sharding import PartitionSpec as P

FILTER_RAW = [math.exp(-(offset - 4) * (offset - 4) / 4.5) for offset in range(9)]
FILTER_TAPS = [value / sum(FILTER_RAW) for value in FILTER_RAW]
HALF_TAPS = FILTER_TAPS[4:]

MESH = pl.DeviceIdType.MESH
F32, BF16 = jnp.float32, jnp.bfloat16


def split(value):
    high = value.astype(BF16)
    return high, (value - high.astype(F32)).astype(BF16)


def band(distance):
    out = jnp.zeros(distance.shape, F32)
    for k in range(5):
        out = jnp.where(distance == k, HALF_TAPS[k], out)
    return out


def lane_roll(value, shift):
    flat = value.reshape(-1, value.shape[-1])
    return pltpu.roll(flat, shift, 1).reshape(value.shape)


def filter_z(ref, index, start, cells):
    out = HALF_TAPS[0] * ref[index, pl.ds(8 + start, cells), :]
    for k in range(1, 5):
        out = out + HALF_TAPS[k] * (
            ref[index, pl.ds(8 + start - k, cells), :] + ref[index, pl.ds(8 + start + k, cells), :]
        )
    return out


def product(high, low, both, width):
    out = jnp.dot(high, both, preferred_element_type=F32)
    return out[:, :width] + out[:, width:] + jnp.dot(
        low, both[:, :width], preferred_element_type=F32)


def rows_kernel(
    snaps, comps, x_ref, w_ref, high_ref, low_ref, gram_ref,
    field, rows_high, rows_low, inner, weight, pack_low, pack_high, side, corner, halo, square, slots,
    load_sem, store_sem, halo_send, halo_recv, gram_send, gram_recv,
):
    cells, width = x_ref.shape[1], x_ref.shape[2]
    half = cells // 2
    gy, gz = lax.axis_index("gy"), lax.axis_index("gz")
    ny, nz = lax.axis_size("gy"), lax.axis_size("gz")

    def gz_at(step):
        return lax.rem(gz + step + nz, nz)

    loads = []
    part = snaps * comps // 4
    for q in range(4):
        loads.append(pltpu.make_async_copy(
            x_ref.at[pl.ds(q * part, part)],
            field.at[pl.ds(q * part, part), pl.ds(8, cells)],
            load_sem.at[q],
        ))
        loads[-1].start()
    load_weight = pltpu.make_async_copy(w_ref, weight, load_sem.at[4])
    load_weight.start()
    side[...] = jnp.zeros_like(side)
    corner[...] = jnp.zeros_like(corner)

    barrier = pltpu.get_barrier_semaphore()
    devices = ny * nz
    mine = gy * nz + gz

    def device_at(step):
        flat = lax.rem(mine + step, devices)
        return flat // nz, lax.rem(flat, nz)

    def greet(step, carry):
        pl.semaphore_signal(barrier, inc=1, device_id=device_at(step), device_id_type=MESH)
        return carry

    lax.fori_loop(1, devices, greet, 0, unroll=devices <= 64)

    lane = lax.broadcasted_iota(jnp.int32, (1, width), 1)
    packed = jnp.zeros((comps * cells, width), F32)
    for s in range(snaps):
        if s % 4 == 0:
            loads[s // 4].wait()
        block = field[pl.ds(comps * s, comps), pl.ds(8, cells), :].reshape(comps * cells, width)
        packed = jnp.where(lane // 8 == s, pltpu.roll(block, (4 + 8 * s) % width, 1), packed)
    packed = packed.reshape(comps, cells, width)
    first, second = packed[:, :half], packed[:, half:]
    left_lanes = (lane % 8 < 4).reshape(1, 1, width)
    pack_high[...] = jnp.where(left_lanes, first, lane_roll(second, 4))
    pack_low[...] = jnp.where(left_lanes, lane_roll(second, width - 4), first)

    pl.semaphore_wait(barrier, devices - 1)

    def remote(src, dst, n, target):
        return pltpu.make_async_remote_copy(
            src_ref=src, dst_ref=dst, send_sem=halo_send.at[n], recv_sem=halo_recv.at[n],
            device_id=target, device_id_type=MESH,
        )

    copies = [
        remote(x_ref.at[:, pl.ds(cells - 4, 4), :], field.at[:, pl.ds(4, 4), :], 0, (gy, gz_at(1))),
        remote(x_ref.at[:, pl.ds(0, 4), :], field.at[:, pl.ds(cells + 8, 4), :], 1, (gy, gz_at(-1))),
    ]
    up = jnp.minimum(gy + 1, ny - 1)
    down = jnp.maximum(gy - 1, 0)
    to_up = [
        remote(pack_high, side.at[0], 2, (up, gz)),
        remote(pack_high.at[:, pl.ds(half - 8, 8)], corner.at[0, 0], 3, (up, gz_at(1))),
        remote(pack_high.at[:, pl.ds(0, 8)], corner.at[0, 1], 4, (up, gz_at(-1))),
    ]
    to_down = [
        remote(pack_low, side.at[1], 5, (down, gz)),
        remote(pack_low.at[:, pl.ds(half - 8, 8)], corner.at[1, 0], 6, (down, gz_at(1))),
        remote(pack_low.at[:, pl.ds(0, 8)], corner.at[1, 1], 7, (down, gz_at(-1))),
    ]

    @pl.when(gy < ny - 1)
    def _():
        for copy in to_up:
            copy.start()

    @pl.when(gy > 0)
    def _():
        for copy in to_down:
            copy.start()

    for copy in copies:
        copy.start()

    load_weight.wait()
    root = jnp.sqrt(weight[...])
    row_i = lax.broadcasted_iota(jnp.int32, (width, width), 0)
    col_i = lax.broadcasted_iota(jnp.int32, (width, width), 1)
    j = row_i % 8
    position = jnp.where(j < 4, j - 4, width + j - 4)
    own_both = jnp.concatenate(split(band(jnp.abs(row_i - col_i)) * root), axis=1)
    halo_both = jnp.concatenate(split(band(jnp.abs(position - col_i)) * root), axis=1)

    deep = cells - 16

    def smooth_inner(s, carry):
        high, low = split(jnp.concatenate(
            [filter_z(field, comps * s + c, 8, deep) for c in range(comps)], axis=0))
        inner[s] = product(high, low, own_both, width)
        return carry

    lax.fori_loop(0, snaps, smooth_inner, 0, unroll=True)

    @pl.when(gy > 0)
    def _():
        for copy in to_up:
            copy.wait_recv()

    @pl.when(gy < ny - 1)
    def _():
        for copy in to_down:
            copy.wait_recv()

    halo[:, pl.ds(0, 8), :] = jnp.where(
        left_lanes, lane_roll(corner[0, 0], width - 4), lane_roll(corner[1, 0], 4))
    halo[:, pl.ds(8, half), :] = jnp.where(left_lanes, side[0], side[1])
    halo[:, pl.ds(8 + half, half), :] = jnp.where(
        left_lanes, lane_roll(side[0], width - 4), lane_roll(side[1], 4))
    halo[:, pl.ds(8 + cells, 8), :] = jnp.where(left_lanes, corner[0, 1], corner[1, 1])
    halo_z = jnp.concatenate([filter_z(halo, c, 0, cells) for c in range(comps)], axis=0)
    halo_high, halo_low = split(halo_z)

    for copy in copies:
        copy.wait_recv()

    def smooth_one(s, carry):
        high, low = split(jnp.concatenate(
            [filter_z(field, comps * s + c, z, 8) for c in range(comps) for z in (0, cells - 8)],
            axis=0))
        edge = product(high, low, own_both, width)
        keep = (lane // 8 == s).astype(F32).astype(BF16)
        smooth = product(halo_high * keep, halo_low * keep, halo_both, width)
        own = []
        for c in range(comps):
            own += [
                edge[16 * c:16 * c + 8], inner[s, pl.ds(deep * c, deep), :],
                edge[16 * c + 8:16 * c + 16],
            ]
        smooth = smooth + jnp.concatenate(own, axis=0)
        high = smooth.astype(BF16)
        rest = smooth - high.astype(F32)
        low = rest.astype(BF16)
        square[s] = (rest * rest).reshape(-1, 8, width).sum(axis=0)
        for n in range(comps * cells // 16):
            rows_high[s, :, pl.ds(width * n, width)] = high[16 * n:16 * n + 16]
            rows_low[s, :, pl.ds(width * n, width)] = low[16 * n:16 * n + 16]
        return carry

    lax.fori_loop(0, snaps, smooth_one, 0, unroll=True)

    stores = [
        pltpu.make_async_copy(rows_high, high_ref, store_sem.at[0]),
        pltpu.make_async_copy(rows_low, low_ref, store_sem.at[1]),
    ]
    for store in stores:
        store.start()

    chunks = comps * cells // 16
    size = snaps * 16
    high = rows_high[...].reshape(size, width * chunks)
    low = rows_low[...].reshape(size, width * chunks)
    dims = (((1,), (1,)), ((), ()))
    big_i = lax.broadcasted_iota(jnp.int32, (size, size), 0)
    big_j = lax.broadcasted_iota(jnp.int32, (size, size), 1)
    same = big_i % 16 == big_j % 16

    def equal_z(left, right):
        big = lax.dot_general(left, right, dims, preferred_element_type=F32)
        return jnp.where(same, big, 0.0).reshape(snaps, 16, size).sum(axis=1)

    main, cross = equal_z(high, high), equal_z(low, high)
    groups = width // snaps
    gather_i = lax.broadcasted_iota(jnp.int32, (size, width), 0)
    gather_j = lax.broadcasted_iota(jnp.int32, (size, width), 1)
    gather = (gather_i // 16 == gather_j % snaps).astype(F32)
    other_i = lax.broadcasted_iota(jnp.int32, (snaps, size), 0)
    other_j = lax.broadcasted_iota(jnp.int32, (snaps, size), 1)
    other = (other_j // 16 == other_i).astype(F32)
    gram = jnp.dot(
        main + cross, gather, precision=lax.Precision.HIGHEST, preferred_element_type=F32)
    gram = gram + lax.dot_general(
        other, jnp.concatenate([cross] * groups, axis=0), dims,
        precision=lax.Precision.HIGHEST, preferred_element_type=F32)
    g_i = lax.broadcasted_iota(jnp.int32, (snaps, width), 0)
    g_j = lax.broadcasted_iota(jnp.int32, (snaps, width), 1)
    squares = jnp.sum(jnp.sum(square[...], axis=1), axis=1, keepdims=True)
    gram = gram + jnp.where(g_j % snaps == g_i, squares, 0.0)
    gram = jnp.where((g_j // snaps + g_i) % groups == 0, gram, 0.0)
    slots[mine] = gram.reshape(snaps // groups, groups, width).sum(axis=1)

    def share(step):
        return pltpu.make_async_remote_copy(
            src_ref=slots.at[mine], dst_ref=slots.at[mine],
            send_sem=gram_send.at[step], recv_sem=gram_recv.at[step],
            device_id=device_at(step), device_id_type=MESH,
        )

    def each(act):
        def body(step, carry):
            act(share(step))
            return carry
        lax.fori_loop(1, devices, body, 0, unroll=devices <= 64)

    each(lambda copy: copy.start())
    each(lambda copy: copy.wait_recv())
    gram_ref[...] = jnp.sum(slots[...], axis=0)

    for store in stores:
        store.wait()
    each(lambda copy: copy.wait_send())
    for copy in copies:
        copy.wait_send()

    @pl.when(gy < ny - 1)
    def _():
        for copy in to_up:
            copy.wait_send()

    @pl.when(gy > 0)
    def _():
        for copy in to_down:
            copy.wait_send()


def modes_kernel(
    snaps, row_total, high_ref, low_ref, gram_ref, modes_ref, factor_ref,
    rows_high, rows_low, modes, factor, load_sem, out_sem,
):
    loads = [
        pltpu.make_async_copy(high_ref, rows_high, load_sem.at[0]),
        pltpu.make_async_copy(low_ref, rows_low, load_sem.at[1]),
    ]
    for load in loads:
        load.start()
    width = gram_ref.shape[1]
    groups = width // snaps
    size = snaps * 16
    chunks = rows_high.shape[2] // width
    m_i = lax.broadcasted_iota(jnp.int32, (snaps, width), 0)
    m_j = lax.broadcasted_iota(jnp.int32, (snaps, width), 1)
    gram = jnp.concatenate([
        pltpu.roll(
            jnp.broadcast_to(gram_ref[n:n + 1, :], (groups, width)), 0, 1,
            stride=snaps, stride_axis=0)
        for n in range(snaps // groups)
    ], axis=0)
    gram = jnp.where(m_j < snaps, gram, 0.0)

    work = jnp.where(m_j == m_i + snaps, 1.0, gram)
    for k in range(snaps - 1):
        column = work[:, k:k + 1]
        factors = jnp.where(m_i[:, :1] > k, column, 0.0) * (1.0 / work[k:k + 1, k:k + 1])
        work = work - factors * work[k:k + 1, :]
    pivots = jnp.sum(jnp.where(m_i == m_j, work, 0.0), axis=1, keepdims=True)
    work = work / jnp.sqrt(pivots)
    upper = jnp.where(m_j >= m_i, work, 0.0) * (1.0 / math.sqrt(row_total))
    factor[...] = upper[:, :snaps]
    copies = [pltpu.make_async_copy(factor, factor_ref, out_sem.at[0])]
    copies[0].start()

    inverse_high, inverse_low = split(work * math.sqrt(row_total))
    spread_i = lax.broadcasted_iota(jnp.int32, (width, size), 0)
    spread_j = lax.broadcasted_iota(jnp.int32, (width, size), 1)
    spread = (spread_i - snaps == spread_j // 16).astype(F32).astype(BF16)

    same_i = lax.broadcasted_iota(jnp.int32, (size, size), 0)
    same_j = lax.broadcasted_iota(jnp.int32, (size, size), 1)
    same = same_i % 16 == same_j % 16

    def blocks(value):
        tall = jnp.broadcast_to(
            value.astype(F32)[:, None, :], (snaps, 16, width)).reshape(size, width).astype(BF16)
        wide = jnp.dot(tall, spread, preferred_element_type=F32)
        return jnp.where(same, wide, 0.0).astype(BF16)

    inverse_high, inverse_low = blocks(inverse_high), blocks(inverse_low)
    for load in loads:
        load.wait()
    parts = out_sem.shape[0] - 1
    for q in range(parts):
        depth = chunks // parts
        for n in range(q * depth, (q + 1) * depth, 2):
            high = rows_high[:, :, pl.ds(width * n, 2 * width)].reshape(size, 2 * width)
            low = rows_low[:, :, pl.ds(width * n, 2 * width)].reshape(size, 2 * width)
            out = jnp.dot(inverse_high, high, preferred_element_type=F32)
            out = out + jnp.dot(inverse_high, low, preferred_element_type=F32)
            out = out + jnp.dot(inverse_low, high, preferred_element_type=F32)
            for m in range(2):
                modes[:, pl.ds(16 * (n + m), 16), :] = out[
                    :, m * width:(m + 1) * width].reshape(snaps, 16, width)
        span = pl.ds(16 * q * depth, 16 * depth)
        copies.append(pltpu.make_async_copy(
            modes.at[:, span], modes_ref.at[:, span], out_sem.at[q + 1]))
        copies[-1].start()
    for copy in copies:
        copy.wait()


def per_device(snapshots, cell_weight):
    snaps, comps, planes, cells, width = snapshots.shape
    comps_all = comps * planes
    ny, nz = lax.axis_size("gy"), lax.axis_size("gz")
    row_total = comps_all * cells * width * ny * nz
    devices = ny * nz
    depth = width * comps_all * cells // 16
    vmem = pl.BlockSpec(memory_space=pltpu.VMEM)
    hbm = pl.BlockSpec(memory_space=pltpu.HBM)
    rows_high, rows_low, gram = pl.pallas_call(
        functools.partial(rows_kernel, snaps, comps_all),
        out_shape=(
            jax.ShapeDtypeStruct((snaps, 16, depth), BF16),
            jax.ShapeDtypeStruct((snaps, 16, depth), BF16),
            jax.ShapeDtypeStruct((snaps * snaps // width, width), F32),
        ),
        in_specs=[hbm, hbm],
        out_specs=(hbm, hbm, vmem),
        scratch_shapes=[
            pltpu.VMEM((snaps * comps_all, cells + 16, width), F32),
            pltpu.VMEM((snaps, 16, depth), BF16),
            pltpu.VMEM((snaps, 16, depth), BF16),
            pltpu.VMEM((snaps, comps_all * (cells - 16), width), F32),
            pltpu.VMEM((1, width), F32),
            pltpu.VMEM((comps_all, cells // 2, width), F32),
            pltpu.VMEM((comps_all, cells // 2, width), F32),
            pltpu.VMEM((2, comps_all, cells // 2, width), F32),
            pltpu.VMEM((2, 2, comps_all, 8, width), F32),
            pltpu.VMEM((comps_all, cells + 16, width), F32),
            pltpu.VMEM((snaps, 8, width), F32),
            pltpu.VMEM((devices, snaps * snaps // width, width), F32),
            pltpu.SemaphoreType.DMA((5,)),
            pltpu.SemaphoreType.DMA((2,)),
            pltpu.SemaphoreType.DMA((8,)),
            pltpu.SemaphoreType.DMA((8,)),
            pltpu.SemaphoreType.DMA((devices,)),
            pltpu.SemaphoreType.DMA((devices,)),
        ],
        compiler_params=pltpu.CompilerParams(
            collective_id=0, has_side_effects=True, vmem_limit_bytes=60 * 1024 * 1024
        ),
    )(snapshots.reshape(snaps * comps_all, cells, width), cell_weight.reshape(1, width))
    modes, factor = pl.pallas_call(
        functools.partial(modes_kernel, snaps, row_total),
        out_shape=(
            jax.ShapeDtypeStruct((snaps, comps_all * cells, width), F32),
            jax.ShapeDtypeStruct((snaps, snaps), F32),
        ),
        in_specs=[hbm, hbm, vmem],
        out_specs=(hbm, hbm),
        scratch_shapes=[
            pltpu.VMEM((snaps, 16, depth), BF16),
            pltpu.VMEM((snaps, 16, depth), BF16),
            pltpu.VMEM((snaps, comps_all * cells, width), F32),
            pltpu.VMEM((snaps, snaps), F32),
            pltpu.SemaphoreType.DMA((2,)),
            pltpu.SemaphoreType.DMA((4,)),
        ],
        compiler_params=pltpu.CompilerParams(vmem_limit_bytes=60 * 1024 * 1024),
    )(rows_high, rows_low, gram)
    return modes.reshape(snapshots.shape), factor


def solution(mesh):
    return jax.shard_map(
        per_device,
        mesh=mesh,
        in_specs=(P(None, None, None, "gz", "gy"), P("gy")),
        out_specs=(P(None, None, None, "gz", "gy"), P()),
        check_vma=False,
    )
```
